256 devices in a mesh: ind: 8 (over x, core), var: 32 (over y, z).
Axes of the slice: x: 4, y: 4, z: 8, core: 2. Of those that a mesh axis runs over, the one named last changes fastest.
Arguments:
- genotypes: bfloat16 [12288, 102400], P('ind', 'var'), may hold values from -0.0546875 to 0.0546875
- phenotype: float32 [12288, 192], P('ind'), may hold values from -40 to 40, as said below
- beta_start: float32 [192, 102400], P('ind', 'var'), may hold values from -5 to 5, as said below
- penalty: float32 [192], replicated, may hold values from 0.5 to 4
- step_size: float32 [1], replicated, may hold values from 0.02 to 0.06
Outputs:
- beta_final: float32 [192, 102400], P('ind', 'var')
- objective: float32 [2, 192], replicated
The draws below stay inside these ranges and needn't reach their ends.
Inputs may be any that keep to these rules, and one draw needn't show every extreme that they name: `phenotype`: Real-valued phenotypes. `beta_start`: Real-valued warm-start coefficients, a part of them exactly zero.
All inputs are finite; a program needn't handle non-finite values.
Results may differ from the reference program's by a relative error of at most 0.00087.
Values may be sent and summed in bfloat16 or wider, within the bound.
A program may use at most 64 MiB of HBM per device.

```python
import math
import jax
import jax.numpy as jnp
from jax import lax

P_SIZE = 102400
TRAITS = 192
ITERS = 2
N = 12288


def draw_phenotype(key, part):
    key = jax.random.fold_in(key, 1)
    row_ramp = 1.0 + 2.0 * jnp.arange(N, dtype=jnp.float32)[:, None] / max(N - 1, 1)
    base = jnp.clip(jax.random.normal(key, (N, TRAITS), jnp.float32), -5.0, 5.0)
    return (base * row_ramp).astype(jnp.float32)


def draw_beta_start(key, part):
    key = jax.random.fold_in(key, 2)
    col_ramp = 1.0 + 2.0 * jnp.arange(P_SIZE, dtype=jnp.float32)[None, :] / max(P_SIZE - 1, 1)
    keep = jax.random.uniform(jax.random.fold_in(key, 3), (TRAITS, P_SIZE), jnp.float32) < 0.6
    values = 0.3 * jnp.clip(jax.random.normal(key, (TRAITS, P_SIZE), jnp.float32), -4.0, 4.0) * col_ramp
    return jnp.where(keep, values, 0.0).astype(jnp.float32)


def block_levels(key, extent, shards, low, top_value):
    level = 1.0
    for position, blocks in shards:
        draws = jax.random.uniform(jax.random.fold_in(jax.random.fold_in(key, 6), position), (blocks,), jnp.float32, low / len(shards), top_value / len(shards))
        level = level * jnp.repeat(jnp.exp(draws), extent[position] // blocks).reshape((-1,) + (1,) * (len(extent) - 1 - position))
    return level


def scatter_about(stream_key, extent, spread, limit, split=(), held_as=jnp.bfloat16):
    result = spread * jax.random.normal(stream_key, extent, jnp.float32)
    if split:
        result = result * block_levels(stream_key, extent, split, -0.22, 0.18)
    return jnp.clip(result, -limit, limit).astype(held_as)


def setup_inputs(seed: int = 0) -> dict:
    splits = jax.random.split(jax.random.key(seed), 6)
    return {
        "genotypes": scatter_about(splits[0], (N, P_SIZE), N ** -0.5, 0.0546875, ((0, 8), (1, 32))),
        "phenotype": draw_phenotype(jax.random.fold_in(splits[5], 71), 0),
        "beta_start": draw_beta_start(jax.random.fold_in(splits[5], 71), 0),
        "penalty": jnp.clip(jnp.exp(jax.random.uniform(splits[3], (TRAITS,), jnp.float32, math.log(0.5), math.log(4.0))), 0.5, 4.0),
        "step_size": jnp.clip(jax.random.uniform(splits[4], (1,), jnp.float32, 0.02, 0.06), 0.02, 0.06),
    }


def reference(genotypes, phenotype, beta_start, penalty, step_size):
    beta = beta_start
    scale = step_size[0]
    records = []
    for iteration in range(ITERS):
        coef_half = beta.astype(jnp.bfloat16)
        predictor = lax.dot_general(genotypes, coef_half, (((1,), (1,)), ((), ())), preferred_element_type=jnp.float32)
        residual = phenotype - predictor
        loss_part = 0.5 * jnp.sum(residual * residual, axis=0)
        penalty_part = penalty * jnp.sum(jnp.abs(beta), axis=1)
        records.append((loss_part + penalty_part) / jnp.float32(N))
        residual_half = residual.astype(jnp.bfloat16)
        ascent = lax.dot_general(residual_half, genotypes, (((0,), (0,)), ((), ())), preferred_element_type=jnp.float32)
        moved = beta + scale * ascent
        beta = jnp.sign(moved) * jnp.maximum(jnp.abs(moved) - scale * penalty[:, None], 0.0)
    return beta, jnp.stack(records, axis=0)
```

```python
import functools

import jax
import jax.numpy as jnp
from jax import lax
from jax.experimental import pallas as pl
from jax.experimental.pallas import tpu as pltpu
from jax.sharding import PartitionSpec as P

ITERS = 2
X, C, Y, Z = 4, 2, 4, 8
GROUPS = 3
R8 = 8
ROWS, COLS = 1536, 3200
TRAITS = 192
LOCAL = TRAITS // (X * C)
GT = R8 * X * C
CHUNK = ROWS // Y
LO = 1664
HI = COLS - LO
MESH = pl.DeviceIdType.MESH
F32, BF16 = jnp.float32, jnp.bfloat16
NT = (((1,), (1,)), ((), ()))
NN = (((1,), (0,)), ((), ()))
COL_CHUNK = 640


def kernel(
    step_ref, pen_ref, geno, pheno, beta0, out_beta, out_obj,
    g_buf, ph_in, ph_t, beta, stat, stat_y, stat_z, stat_x, stat_c,
    cb, coef, pp, ry, sz, rz, az, rt, gp, pr, ps, rx,
    load_sem,
    agx_s, agx_r, rel_s, rel_r, rsy_s, rsy_r, rsz_s, rsz_r, agz_s, agz_r, agy_s, agy_r, pair_s, pair_r, rsx_s, rsx_r,
    ob_s, ob_r,
):
    ind, var = lax.axis_index("ind"), lax.axis_index("var")
    x, c = ind // C, ind % C
    y, z = var // Z, var % Z

    def at_x(k):
        return (((x + k) % X) * C + c, var)

    def at_y(k):
        return (ind, ((y + k) % Y) * Z + z)

    def at_z(k):
        return (ind, y * Z + (z + k) % Z)

    peer = (x * C + (1 - c), var)

    loads = []
    beta_load = pltpu.make_async_copy(beta0, beta, load_sem.at[0])
    beta_load.start()
    for n, k in enumerate((2, 1, 3, 0)):
        rows = pl.ds(pl.multiple_of(((y + k) % Y) * CHUNK, CHUNK), CHUNK)
        load = pltpu.make_async_copy(geno.at[rows, :], g_buf.at[pl.ds(k * CHUNK, CHUNK), :], load_sem.at[2 + n])
        loads.append(load)
    loads[0].start()
    rows = pl.ds(pl.multiple_of(y * CHUNK, CHUNK), CHUNK)
    ph_load = pltpu.make_async_copy(pheno.at[rows, :], ph_in, load_sem.at[1])
    ph_load.start()
    for load in loads[1:]:
        load.start()

    barrier = pltpu.get_barrier_semaphore()
    partners = [peer]
    partners += [at_x(k) for k in range(1, X)] + [at_y(k) for k in range(1, Y)] + [at_z(k) for k in range(1, Z)]
    for partner in partners:
        pl.semaphore_signal(barrier, inc=1, device_id=partner, device_id_type=MESH)
    pl.semaphore_wait(barrier, len(partners))

    scale = step_ref[0]
    lane = lax.broadcasted_iota(jnp.int32, (LOCAL, TRAITS), 1)
    row = lax.broadcasted_iota(jnp.int32, (LOCAL, TRAITS), 0)
    mine = lane == row + ind * LOCAL
    pen_col = jnp.sum(jnp.where(mine, pen_ref[...], 0.0), axis=1, keepdims=True)
    stat[...] = jnp.zeros_like(stat)
    s_lane = lax.broadcasted_iota(jnp.int32, (R8, 256), 1)
    s_row = lax.broadcasted_iota(jnp.int32, (R8, 256), 0)

    def add_stat(it, first, column):
        hit = s_lane == s_row + first
        stat[it : it + 1, :] += jnp.sum(jnp.where(hit, column, 0.0), axis=0, keepdims=True) * (1.0 / (ROWS * X * C))

    pending = {}

    def send(key, src, dst, s_sem, r_sem, device):
        copy = pltpu.make_async_remote_copy(
            src_ref=src, dst_ref=dst, send_sem=s_sem, recv_sem=r_sem, device_id=device, device_id_type=MESH
        )
        copy.start()
        pending.setdefault(key, []).append(copy)

    def receive(key, one=None):
        copies = pending[key] if one is None else [pending[key][one]]
        for copy in copies:
            copy.wait_recv()

    def settle(key):
        for copy in pending.pop(key, []):
            copy.wait_send()

    def send_coef(g, it):
        settle(("agx", g))
        b = beta[R8 * g : R8 * g + R8, :]
        add_stat(it, ind * LOCAL + R8 * g, pen_col[R8 * g : R8 * g + R8] * jnp.sum(jnp.abs(b), axis=1, keepdims=True))
        high = jnp.concatenate([b[:, LO:], jnp.zeros((R8, LO - HI), F32)], axis=1)
        cb[g, 0, 0] = jnp.concatenate([b[:, :LO], high], axis=0).astype(BF16)
        own = cb.at[g, 0, 0]
        for n, k in enumerate((2, 1, 3)):
            send(("agx", g), own, cb.at[g, k, 0], agx_s.at[g, n], agx_r.at[g, n], at_x(k))
        send(("agx", g), own, cb.at[g, 0, 1], agx_s.at[g, 3], agx_r.at[g, 3], peer)

    def t0(g, it):
        if g == 0:
            beta_load.wait()
        send_coef(g, 0)

    def t1(g, it):
        for n, k in ((1, 1), (2, 3), (0, 2)):
            receive(("agx", g), n)
            send(("rel", g), cb.at[g, k, 0], cb.at[g, k, 1], rel_s.at[g, k - 1], rel_r.at[g, k - 1], peer)

    def t2(g, it):
        receive(("agx", g), 3)
        receive(("rel", g))
        settle(("rsy", g))
        for k in range(X):
            a, b = cb[g, k, 0].astype(F32), cb[g, k, 1].astype(F32)
            rows = slice(2 * R8 * k, 2 * R8 * k + 2 * R8)
            coef[rows, :LO] = jnp.concatenate([a[:R8], b[:R8]], axis=0).astype(BF16)
            coef[rows, LO:] = jnp.concatenate([a[R8:, :HI], b[R8:, :HI]], axis=0).astype(BF16)
        for n, k in enumerate((2, 1, 3, 0)):
            if it == 0 and g == 0:
                loads[n].wait()
            pp[g, k] = lax.dot_general(
                coef[...], g_buf[CHUNK * k : CHUNK * k + CHUNK, :], NT, preferred_element_type=F32
            )
            if k:
                send(("rsy", g), pp.at[g, k], ry.at[g, k - 1], rsy_s.at[g, k - 1], rsy_r.at[g, k - 1], at_y(k))

    def t3(g, it):
        receive(("rsy", g))
        settle(("rsz", g))
        total = pp[g, 0] + ry[g, 0] + ry[g, 1] + ry[g, 2]
        sz[g] = total.reshape(Z, R8, CHUNK)
        for k in (4, 3, 5, 2, 6, 1, 7):
            send(("rsz", g), sz.at[g, (z + k) % Z], rz.at[g, k - 1], rsz_s.at[g, k - 1], rsz_r.at[g, k - 1], at_z(k))

    def t4(g, it):
        if it == 0 and g == 0:
            ph_load.wait()
            ph_t[...] = ph_in[...].T.reshape(X * C * GROUPS, R8, CHUNK)
        receive(("rsz", g))
        settle(("agz", g))
        total = sz[g, z]
        for k in range(Z - 1):
            total += rz[g, k]
        k, f = z // C, z % C
        owner = ((x - k + X) % X) * C + (c + f) % C
        residual = ph_t[owner * GROUPS + g] - total
        az[g, z] = residual
        add_stat(it, owner * LOCAL + R8 * g, 0.5 * jnp.sum(residual * residual, axis=1, keepdims=True))
        for k in (4, 3, 5, 2, 6, 1, 7):
            send(("agz", g), az.at[g, z], az.at[g, z], agz_s.at[g, k - 1], agz_r.at[g, k - 1], at_z(k))

    def t5(g, it):
        receive(("agz", g))
        settle(("agy", g))
        rt[g, :, :CHUNK] = az[g].reshape(GT, CHUNK).astype(BF16)
        for k in (2, 1, 3):
            m = (Y - k) % Y
            send(
                ("agy", g), rt.at[g, :, pl.ds(0, CHUNK)], rt.at[g, :, pl.ds(m * CHUNK, CHUNK)],
                agy_s.at[g, k - 1], agy_r.at[g, k - 1], at_y(k),
            )

    def t6(g, it):
        receive(("agy", g))
        settle(("pair", g))
        for s in range(0, COLS, COL_CHUNK):
            part = lax.dot_general(rt[g], g_buf[:, s : s + COL_CHUNK], NN, preferred_element_type=F32)
            gp[g, :, :, :, s : s + COL_CHUNK] = part.reshape(X, C, R8, COL_CHUNK)
        send(("pair", g), gp.at[g, :, 1], pr.at[g], pair_s.at[g], pair_r.at[g], peer)

    def t7(g, it):
        receive(("pair", g))
        settle(("rel", g))
        settle(("rsx", g))
        for k in (2, 1, 3, 0):
            ps[g, k] = gp[g, k, 0] + pr[g, k]
            if k:
                send(("rsx", g), ps.at[g, k], rx.at[g, k - 1], rsx_s.at[g, k - 1], rsx_r.at[g, k - 1], at_x(X - k))

    def t8(g, it):
        receive(("rsx", g))
        ascent = ps[g, 0] + rx[g, 0] + rx[g, 1] + rx[g, 2]
        rows = slice(R8 * g, R8 * g + R8)
        moved = beta[rows, :] + scale * ascent
        bound = scale * pen_col[rows]
        updated = moved - jnp.clip(moved, -bound, bound)
        if it == ITERS - 1:
            out_beta[rows, :] = updated
        else:
            beta[rows, :] = updated
            send_coef(g, it + 1)

    def o1():
        stat_y[y] = stat[...]
        for k in range(1, Y):
            send("oy", stat_y.at[y], stat_y.at[y], ob_s.at[k - 1], ob_r.at[k - 1], at_y(k))

    def o2():
        receive("oy")
        stat_z[z] = stat_y[0] + stat_y[1] + stat_y[2] + stat_y[3]
        for k in range(1, Z):
            send("oz", stat_z.at[z], stat_z.at[z], ob_s.at[2 + k], ob_r.at[2 + k], at_z(k))

    def o3():
        receive("oz")
        total = stat_z[0]
        for k in range(1, Z):
            total += stat_z[k]
        stat_x[x] = total
        for k in range(1, X):
            send("ox", stat_x.at[x], stat_x.at[x], ob_s.at[9 + k], ob_r.at[9 + k], at_x(k))

    def o4():
        receive("ox")
        stat_c[c] = stat_x[0] + stat_x[1] + stat_x[2] + stat_x[3]
        send("oc", stat_c.at[c], stat_c.at[c], ob_s.at[13], ob_r.at[13], peer)

    def o5():
        receive("oc")
        total = stat_c[0] + stat_c[1]
        out_obj[...] = total[:ITERS, :TRAITS]

    stages = [t1, t2, t3, t4, t5, t6, t7, t8]
    for g in range(GROUPS):
        t0(g, 0)
    count = ITERS * len(stages)
    objective = [o1, o2, o3, o4, o5]
    last_t4 = (ITERS - 1) * len(stages) + 3
    lag = LAG
    for slot in range(count + lag * (GROUPS - 1)):
        for g in range(GROUPS):
            n = slot - lag * g
            if 0 <= n < count:
                stages[n % len(stages)](g, n // len(stages))
        if slot >= last_t4 + lag * (GROUPS - 1) and objective:
            objective.pop(0)()
    while objective:
        objective.pop(0)()
    for key in list(pending):
        settle(key)


LAG = 3


def on_device(genotypes, phenotype, beta_start, penalty, step_size):
    vmem, smem, hbm = (pl.BlockSpec(memory_space=m) for m in (pltpu.VMEM, pltpu.SMEM, pl.ANY))
    dma = pltpu.SemaphoreType.DMA

    def buf(*shape, dtype=F32):
        return pltpu.VMEM(shape, dtype)

    def pairs(*shape):
        return [dma(shape), dma(shape)]

    n = GROUPS
    return pl.pallas_call(
        kernel,
        name="lasso_steps",
        out_shape=(
            jax.ShapeDtypeStruct((LOCAL, COLS), F32),
            jax.ShapeDtypeStruct((ITERS, TRAITS), F32),
        ),
        in_specs=[smem, vmem, hbm, hbm, hbm],
        out_specs=(vmem, vmem),
        scratch_shapes=[
            buf(ROWS, COLS, dtype=BF16),
            buf(CHUNK, TRAITS),
            buf(X * C * n, R8, CHUNK),
            buf(LOCAL, COLS),
            buf(R8, 256),
            buf(Y, R8, 256),
            buf(Z, R8, 256),
            buf(X, R8, 256),
            buf(C, R8, 256),
            buf(n, X, C, 2 * R8, LO, dtype=BF16),
            buf(GT, COLS, dtype=BF16),
            buf(n, Y, GT, CHUNK),
            buf(n, Y - 1, GT, CHUNK),
            buf(n, Z, R8, CHUNK),
            buf(n, Z - 1, R8, CHUNK),
            buf(n, Z, R8, CHUNK),
            buf(n, GT, ROWS, dtype=BF16),
            buf(n, X, C, R8, COLS),
            buf(n, X, R8, COLS),
            buf(n, X, R8, COLS),
            buf(n, X - 1, R8, COLS),
            dma((6,)),
            *pairs(n, X),
            *pairs(n, X - 1),
            *pairs(n, Y - 1),
            *pairs(n, Z - 1),
            *pairs(n, Z - 1),
            *pairs(n, Y - 1),
            *pairs(n),
            *pairs(n, X - 1),
            *pairs(14),
        ],
        compiler_params=pltpu.CompilerParams(
            collective_id=1, has_side_effects=True, vmem_limit_bytes=40 * 1024 * 1024
        ),
        cost_estimate=pl.CostEstimate(flops=4 * 2 * ROWS * COLS * TRAITS, bytes_accessed=12000000, transcendentals=0),
    )(step_size, penalty.reshape(1, TRAITS), genotypes, phenotype, beta_start)


def solution(mesh):
    placed = (P("ind", "var"), P("ind", None), P("ind", "var"), P(), P())
    return jax.shard_map(
        on_device, mesh=mesh, in_specs=placed, out_specs=(P("ind", "var"), P()), check_vma=False
    )
```

```python
import functools

import jax
import jax.numpy as jnp
from jax import lax
from jax.experimental import pallas as pl
from jax.experimental.pallas import tpu as pltpu
from jax.sharding import PartitionSpec as P

ITERS = 2
X, C, Y, Z = 4, 2, 4, 8
GROUPS = 3
R8 = 8
ROWS, COLS = 1536, 3200
TRAITS = 192
LOCAL = TRAITS // (X * C)
GT = R8 * X * C
CHUNK = ROWS // Y
LO = 1664
HI = COLS - LO
PACK = 2 * R8
MESH = pl.DeviceIdType.MESH
F32, BF16 = jnp.float32, jnp.bfloat16
NT = (((1,), (1,)), ((), ()))
NN = (((1,), (0,)), ((), ()))
NEAR_Z = (4, 3, 5, 2, 6, 1, 7)
ORDER = (
    0, 0, 1, 0, 0, 1, 0, 0, 1, 1, 1, 2, 0, 1, 2, 2, 2, 0, 2, 1, 2, 0, 0, 1, 0, 0, 2, 0,
    1, 1, 1, 1, 2, 1, 0, 2, 2, 2, 2, 1, 2, 0, 0, 0, 0, 1, 0, 1, 2, 1, 0, 1, 1, 2, 1, 2,
    2, 2, 1, 2, 2, 0, 1, 2, 0, 1, 1, 1, 1, 2, 0, 0, 0, 1, 0, 2, 2, 2, 2, 0, 1, 2, 0, 2,
)


def kernel(
    step_ref, pen_ref, geno, pheno, beta0, out_beta, out_obj,
    g_buf, ph_t, bp, stat, stat_y, stat_z, stat_x, stat_c,
    cb, coef, pp, pph, ry, ryh, sz, rz, az, rt, keep, gp, pr, ps, psh, rx, rxh, asc,
    load_sem,
    agx_s, agx_r, rel_s, rel_r, rsy_s, rsy_r, rsz_s, rsz_r, agz_s, agz_r, agy_s, agy_r, pair_s, pair_r, rsx_s, rsx_r,
    ob_s, ob_r,
):
    ind, var = lax.axis_index("ind"), lax.axis_index("var")
    x, c = ind // C, ind % C
    y, z = var // Z, var % Z

    def at_x(k):
        return (((x + k) % X) * C + c, var)

    def at_y(k):
        return (ind, ((y + k) % Y) * Z + z)

    def at_z(k):
        return (ind, y * Z + (z + k) % Z)

    peer = (x * C + (1 - c), var)

    beta_loads = [
        pltpu.make_async_copy(beta0.at[:, :, pl.ds(0, LO)], bp.at[:, pl.ds(0, R8), :], load_sem.at[0]),
        pltpu.make_async_copy(beta0.at[:, :, pl.ds(LO, HI)], bp.at[:, pl.ds(R8, R8), pl.ds(0, HI)], load_sem.at[1]),
    ]
    for load in beta_loads:
        load.start()
    loads = []
    for n, k in enumerate((2, 1, 3, 0)):
        rows = pl.ds(pl.multiple_of(((y + k) % Y) * CHUNK, CHUNK), CHUNK)
        loads.append(pltpu.make_async_copy(geno.at[rows, :], g_buf.at[pl.ds(k * CHUNK, CHUNK), :], load_sem.at[3 + n]))
    for load in loads:
        load.start()
    own = pl.ds(pl.multiple_of(y * CHUNK, CHUNK), CHUNK)
    ph_load = pltpu.make_async_copy(pheno.at[:, own], ph_t, load_sem.at[2])
    ph_load.start()

    barrier = pltpu.get_barrier_semaphore()
    partners = [peer]
    partners += [at_x(k) for k in range(1, X)] + [at_y(k) for k in range(1, Y)] + [at_z(k) for k in range(1, Z)]
    for partner in partners:
        pl.semaphore_signal(barrier, inc=1, device_id=partner, device_id_type=MESH)

    scale = step_ref[0]
    bp[:, R8:, HI:] = jnp.zeros((GROUPS, R8, LO - HI), F32)
    for g in range(GROUPS):
        gp[g, :, :, R8:, HI:] = jnp.zeros((X, C, R8, LO - HI), F32)
    stat[...] = jnp.zeros_like(stat)

    pending = {}
    loaded = [False] * Y
    ph_loaded = []

    def send(key, src, dst, s_sem, r_sem, device):
        copy = pltpu.make_async_remote_copy(
            src_ref=src, dst_ref=dst, send_sem=s_sem, recv_sem=r_sem, device_id=device, device_id_type=MESH
        )
        copy.start()
        pending.setdefault(key, []).append(copy)

    def receive(key, one=None):
        copies = pending[key] if one is None else [pending[key][one]]
        for copy in copies:
            copy.wait_recv()

    def settle(key):
        for copy in pending.pop(key, []):
            copy.wait_send()

    for load in beta_loads:
        load.wait()
    pl.semaphore_wait(barrier, len(partners))

    def send_coef(g):
        settle(("agx", g))
        cb[g, 0, 0] = bp[g].astype(BF16)
        own = cb.at[g, 0, 0]
        for m, k in enumerate((2, 1, 3)):
            send(("agx", g), own, cb.at[g, k, 0], agx_s.at[g, m], agx_r.at[g, m], at_x(k))
        send(("agx", g), own, cb.at[g, 0, 1], agx_s.at[g, 3], agx_r.at[g, 3], peer)

    for g in range(GROUPS):
        send_coef(g)

    lane = lax.broadcasted_iota(jnp.int32, (LOCAL, TRAITS), 1)
    row = lax.broadcasted_iota(jnp.int32, (LOCAL, TRAITS), 0)
    pen_col = jnp.sum(jnp.where(lane == row + ind * LOCAL, pen_ref[...], 0.0), axis=1, keepdims=True)
    s_lane = lax.broadcasted_iota(jnp.int32, (LOCAL, 256), 1)
    s_row = lax.broadcasted_iota(jnp.int32, (LOCAL, 256), 0)

    def add_stat(it, first, column):
        hit = s_lane[: column.shape[0]] == s_row[: column.shape[0]] + first
        stat[it : it + 1, :] += jnp.sum(jnp.where(hit, column, 0.0), axis=0, keepdims=True) * (1.0 / (ROWS * X * C))

    def add_penalty(g, it):
        size = jnp.sum(jnp.abs(bp[g]), axis=1, keepdims=True)
        first = R8 * g
        add_stat(it, ind * LOCAL + first, pen_col[first : first + R8] * (size[:R8] + size[R8:]))

    def t1(g, it):
        for m, k in ((1, 1), (2, 3), (0, 2)):
            receive(("agx", g), m)
            send(("rel", g), cb.at[g, k, 0], cb.at[g, k, 1], rel_s.at[g, m], rel_r.at[g, m], peer)
        add_penalty(g, it)

    def t2(n, g, it):
        if n == 0:
            receive(("agx", g), 3)
            receive(("rel", g))
            settle(("rsy", g))
            for k in range(X):
                a, b = cb[g, k, 0].astype(F32), cb[g, k, 1].astype(F32)
                rows = slice(2 * R8 * k, 2 * R8 * k + 2 * R8)
                coef[g, rows, :LO] = jnp.concatenate([a[:R8], b[:R8]], axis=0).astype(BF16)
                coef[g, rows, LO:] = jnp.concatenate([a[R8:, :HI], b[R8:, :HI]], axis=0).astype(BF16)
        k = (2, 1, 3, 0)[n]
        if it == 0 and not loaded[n]:
            loads[n].wait()
            loaded[n] = True
        mine = lax.dot_general(
            coef[g], g_buf[CHUNK * k : CHUNK * k + CHUNK, :], NT, preferred_element_type=F32
        )
        if it:
            mine = mine - pp[g, k]
        if it and k:
            pph[g, k - 1] = mine.astype(BF16)
        else:
            pp[g, k] = mine
        if k:
            src, dst = (pph.at[g, k - 1], ryh.at[g, k - 1]) if it else (pp.at[g, k], ry.at[g, k - 1])
            send(("rsy", g), src, dst, rsy_s.at[g, k - 1], rsy_r.at[g, k - 1], at_y(k))

    def t3(g, it):
        receive(("rsy", g))
        settle(("rsz", g))
        total = pp[g, 0]
        for k in range(Y - 1):
            total = total + (ryh[g, k].astype(F32) if it else ry[g, k])
        sz[g] = total.reshape(Z, R8, CHUNK)
        for k in NEAR_Z:
            send(("rsz", g), sz.at[g, (z + k) % Z], rz.at[g, k - 1], rsz_s.at[g, k - 1], rsz_r.at[g, k - 1], at_z(k))

    def t4(g, it):
        if it == 0 and not ph_loaded:
            ph_load.wait()
            ph_loaded.append(True)
        receive(("rsz", g))
        settle(("agz", g))
        total = sz[g, z]
        for k in range(Z - 1):
            total = total + rz[g, k]
        if it:
            total = total + keep[g]
        else:
            keep[g] = total
        k, f = z // C, z % C
        owner = ((x - k + X) % X) * C + (c + f) % C
        first = owner * LOCAL + R8 * g
        residual = ph_t[pl.ds(pl.multiple_of(first, R8), R8), :] - total
        az[g, z] = residual
        for k in NEAR_Z:
            send(("agz", g), az.at[g, z], az.at[g, z], agz_s.at[g, k - 1], agz_r.at[g, k - 1], at_z(k))
        add_stat(it, first, 0.5 * jnp.sum(residual * residual, axis=1, keepdims=True))

    def t5(g, it):
        receive(("agz", g))
        settle(("agy", g))
        rt[g, :, :CHUNK] = az[g].reshape(GT, CHUNK).astype(BF16)
        for k in (2, 1, 3):
            m = (Y - k) % Y
            send(
                ("agy", g), rt.at[g, :, pl.ds(0, CHUNK)], rt.at[g, :, pl.ds(m * CHUNK, CHUNK)],
                agy_s.at[g, k - 1], agy_r.at[g, k - 1], at_y(k),
            )

    def t6(n, g, it):
        if n == 0:
            receive(("agy", g))
            settle(("pair", g))
        row, a, b = ((0, 0, 896), (0, 896, LO), (1, 0, 768), (1, 768, HI))[n]
        part = lax.dot_general(rt[g], g_buf[:, LO * row + a : LO * row + b], NN, preferred_element_type=F32)
        gp[g, :, :, R8 * row : R8 * row + R8, a:b] = part.reshape(X, C, R8, b - a)
        if n == 3:
            send(("pair", g), gp.at[g, :, 1], pr.at[g], pair_s.at[g], pair_r.at[g], peer)

    def t7(g, it):
        receive(("pair", g))
        settle(("rel", g))
        settle(("rsx", g))
        for k in (2, 1, 3, 0):
            mine = gp[g, k, 0] + pr[g, k]
            if it:
                mine = mine - ps[g, k]
            if it and k:
                psh[g, k - 1] = mine.astype(BF16)
            else:
                ps[g, k] = mine
            if k:
                src, dst = (psh.at[g, k - 1], rxh.at[g, k - 1]) if it else (ps.at[g, k], rx.at[g, k - 1])
                send(("rsx", g), src, dst, rsx_s.at[g, k - 1], rsx_r.at[g, k - 1], at_x(X - k))

    def t8(g, it):
        receive(("rsx", g))
        ascent = ps[g, 0]
        for k in range(X - 1):
            ascent = ascent + (rxh[g, k].astype(F32) if it else rx[g, k])
        if it:
            ascent = ascent + asc[g]
        else:
            asc[g] = ascent
        rows = slice(R8 * g, R8 * g + R8)
        moved = bp[g] + scale * ascent
        bound = jnp.concatenate([pen_col[rows], pen_col[rows]], axis=0) * scale
        updated = moved - jnp.clip(moved, -bound, bound)
        if it == ITERS - 1:
            out_beta[rows, :LO] = updated[:R8]
            out_beta[rows, LO:] = updated[R8:, :HI]
        else:
            bp[g] = updated
            send_coef(g)

    def o1():
        stat_y[y] = stat[...]
        for k in range(1, Y):
            send("oy", stat_y.at[y], stat_y.at[y], ob_s.at[k - 1], ob_r.at[k - 1], at_y(k))

    def o2():
        receive("oy")
        stat_z[z] = stat_y[0] + stat_y[1] + stat_y[2] + stat_y[3]
        for k in range(1, Z):
            send("oz", stat_z.at[z], stat_z.at[z], ob_s.at[2 + k], ob_r.at[2 + k], at_z(k))

    def o3():
        receive("oz")
        total = stat_z[0]
        for k in range(1, Z):
            total = total + stat_z[k]
        stat_x[x] = total
        for k in range(1, X):
            send("ox", stat_x.at[x], stat_x.at[x], ob_s.at[9 + k], ob_r.at[9 + k], at_x(k))

    def o4():
        receive("ox")
        stat_c[c] = stat_x[0] + stat_x[1] + stat_x[2] + stat_x[3]
        send("oc", stat_c.at[c], stat_c.at[c], ob_s.at[13], ob_r.at[13], peer)

    def o5():
        receive("oc")
        out_obj[...] = (stat_c[0] + stat_c[1])[:ITERS, :TRAITS]

    stages = []
    for it in range(ITERS):
        stages += [(t1, it)] + [(functools.partial(t2, n), it) for n in range(Y)]
        stages += [(t3, it), (t4, it), (t5, it)] + [(functools.partial(t6, n), it) for n in range(4)] + [(t7, it), (t8, it)]
    objective = [o1, o2, o3, o4, o5]
    done = [0] * GROUPS
    for place, g in enumerate(ORDER):
        stage, it = stages[done[g]]
        stage(g, it)
        done[g] += 1
        if min(done) > stages.index((t4, ITERS - 1)) and objective and place % 3 == 0:
            objective.pop(0)()
    for step in objective:
        step()
    for key in list(pending):
        settle(key)


def on_device(genotypes, phenotype, beta_start, penalty, step_size):
    vmem, smem, hbm = (pl.BlockSpec(memory_space=m) for m in (pltpu.VMEM, pltpu.SMEM, pl.ANY))
    dma = pltpu.SemaphoreType.DMA

    def buf(*shape, dtype=F32):
        return pltpu.VMEM(shape, dtype)

    def pairs(*shape):
        return [dma(shape), dma(shape)]

    n = GROUPS
    return pl.pallas_call(
        kernel,
        name="lasso_steps",
        out_shape=(
            jax.ShapeDtypeStruct((LOCAL, COLS), F32),
            jax.ShapeDtypeStruct((ITERS, TRAITS), F32),
        ),
        in_specs=[smem, vmem, hbm, hbm, hbm],
        out_specs=(vmem, vmem),
        scratch_shapes=[
            buf(ROWS, COLS, dtype=BF16),
            buf(TRAITS, CHUNK),
            buf(n, PACK, LO),
            buf(R8, 256),
            buf(Y, R8, 256),
            buf(Z, R8, 256),
            buf(X, R8, 256),
            buf(C, R8, 256),
            buf(n, X, C, PACK, LO, dtype=BF16),
            buf(n, GT, COLS, dtype=BF16),
            buf(n, Y, GT, CHUNK),
            buf(n, Y - 1, GT, CHUNK, dtype=BF16),
            buf(n, Y - 1, GT, CHUNK),
            buf(n, Y - 1, GT, CHUNK, dtype=BF16),
            buf(n, Z, R8, CHUNK),
            buf(n, Z - 1, R8, CHUNK),
            buf(n, Z, R8, CHUNK),
            buf(n, GT, ROWS, dtype=BF16),
            buf(n, R8, CHUNK),
            buf(n, X, C, PACK, LO),
            buf(n, X, PACK, LO),
            buf(n, X, PACK, LO),
            buf(n, X - 1, PACK, LO, dtype=BF16),
            buf(n, X - 1, PACK, LO),
            buf(n, X - 1, PACK, LO, dtype=BF16),
            buf(n, PACK, LO),
            dma((7,)),
            *pairs(n, X),
            *pairs(n, X - 1),
            *pairs(n, Y - 1),
            *pairs(n, Z - 1),
            *pairs(n, Z - 1),
            *pairs(n, Y - 1),
            *pairs(n),
            *pairs(n, X - 1),
            *pairs(14),
        ],
        compiler_params=pltpu.CompilerParams(
            collective_id=1, has_side_effects=True, vmem_limit_bytes=55 * 1024 * 1024
        ),
        cost_estimate=pl.CostEstimate(flops=4 * 2 * ROWS * COLS * TRAITS, bytes_accessed=12000000, transcendentals=0),
    )(step_size, penalty.reshape(1, TRAITS), genotypes, phenotype.T, beta_start.reshape(n, R8, COLS))


def solution(mesh):
    placed = (P("ind", "var"), P("ind", None), P("ind", "var"), P(), P())
    return jax.shard_map(
        on_device, mesh=mesh, in_specs=placed, out_specs=(P("ind", "var"), P()), check_vma=False
    )
```

```python
import functools

import jax
import jax.numpy as jnp
from jax import lax
from jax.experimental import pallas as pl
from jax.experimental.pallas import tpu as pltpu
from jax.sharding import PartitionSpec as P

ITERS = 2
X, C, Y, Z = 4, 2, 4, 8
GROUPS = 3
R8 = 8
ROWS, COLS = 1536, 3200
TRAITS = 192
LOCAL = TRAITS // (X * C)
GT = R8 * X * C
CHUNK = ROWS // Y
LO = 1664
HI = COLS - LO
PACK = 2 * R8
CUTS = ((0, 896), (896, LO))
MESH = pl.DeviceIdType.MESH
F32, BF16 = jnp.float32, jnp.bfloat16
NT = (((1,), (1,)), ((), ()))
NN = (((1,), (0,)), ((), ()))
NEAR_Z = (4, 3, 5, 2, 6, 1, 7)
ORDER = (
    0, 0, 1, 0, 1, 0, 0, 0, 2, 2, 1, 0, 2, 2, 1, 2, 2, 0, 1, 1, 2, 1, 0, 2, 0, 0, 0, 1, 0, 0, 2, 0, 1, 0,
    2, 2, 2, 0, 2, 2, 0, 1, 2, 1, 0, 1, 1, 1, 2, 0, 2, 1, 0, 1, 0, 0, 2, 2, 0, 1, 2, 1, 2, 2, 2, 1, 0, 2,
    1, 1, 1, 1, 0, 1, 2, 0, 0, 0, 0, 1, 0, 0, 2, 0, 1, 0, 2, 2, 2, 2, 2, 1, 1, 2, 1, 1, 1, 2, 1, 2, 1, 1,
)


def kernel(
    step_ref, pen_ref, geno, pheno, beta0, out_beta, out_obj,
    g_buf, ph_t, bp, stat, stat_y, stat_z, stat_x, stat_c,
    cb, coef, pp, pph, ry, ryh, sz, rz, az, rt, keep, gp, pr, ps, psh, rx, rxh, asc,
    load_sem,
    agx_s, agx_r, rel_s, rel_r, rsy_s, rsy_r, rsz_s, rsz_r, agz_s, agz_r, agy_s, agy_r, pair_s, pair_r, rsx_s, rsx_r,
    ob_s, ob_r,
):
    ind, var = lax.axis_index("ind"), lax.axis_index("var")
    x, c = ind // C, ind % C
    y, z = var // Z, var % Z

    def at_x(k):
        return (((x + k) % X) * C + c, var)

    def at_y(k):
        return (ind, ((y + k) % Y) * Z + z)

    def at_z(k):
        return (ind, y * Z + (z + k) % Z)

    peer = (x * C + (1 - c), var)

    beta_loads = [
        pltpu.make_async_copy(beta0.at[:, :, pl.ds(0, LO)], bp.at[:, pl.ds(0, R8), :], load_sem.at[0]),
        pltpu.make_async_copy(beta0.at[:, :, pl.ds(LO, HI)], bp.at[:, pl.ds(R8, R8), pl.ds(0, HI)], load_sem.at[1]),
    ]
    for load in beta_loads:
        load.start()
    loads = []
    for n, k in enumerate((2, 1, 3, 0)):
        rows = pl.ds(pl.multiple_of(((y + k) % Y) * CHUNK, CHUNK), CHUNK)
        loads.append(pltpu.make_async_copy(geno.at[rows, :], g_buf.at[pl.ds(k * CHUNK, CHUNK), :], load_sem.at[3 + n]))
    own = pl.ds(pl.multiple_of(y * CHUNK, CHUNK), CHUNK)
    ph_load = pltpu.make_async_copy(pheno.at[:, own], ph_t, load_sem.at[2])
    ph_load.start()

    barrier = pltpu.get_barrier_semaphore()
    partners = [peer]
    partners += [at_x(k) for k in range(1, X)] + [at_y(k) for k in range(1, Y)] + [at_z(k) for k in range(1, Z)]
    for partner in partners:
        pl.semaphore_signal(barrier, inc=1, device_id=partner, device_id_type=MESH)

    scale = step_ref[0]
    bp[:, R8:, HI:] = jnp.zeros((GROUPS, R8, LO - HI), F32)
    for g in range(GROUPS):
        gp[g, :, :, R8:, HI:] = jnp.zeros((X, C, R8, LO - HI), F32)
    stat[...] = jnp.zeros_like(stat)

    pending = {}
    loaded = [False] * Y
    ph_loaded = []

    def send(key, src, dst, s_sem, r_sem, device):
        copy = pltpu.make_async_remote_copy(
            src_ref=src, dst_ref=dst, send_sem=s_sem, recv_sem=r_sem, device_id=device, device_id_type=MESH
        )
        copy.start()
        pending.setdefault(key, []).append(copy)

    def receive(key, one=None):
        copies = pending[key] if one is None else [pending[key][one]]
        for copy in copies:
            copy.wait_recv()

    def settle(key):
        for copy in pending.pop(key, []):
            copy.wait_send()

    for load in beta_loads:
        load.wait()
    pl.semaphore_wait(barrier, len(partners))

    def send_coef(n, g):
        settle(("agx", g, n))
        a, b = CUTS[n]
        cols = pl.ds(a, b - a)
        cb[g, 0, 0, :, a:b] = bp[g, :, a:b].astype(BF16)
        own = cb.at[g, 0, 0, :, cols]
        for m, k in enumerate((2, 1, 3)):
            send(("agx", g, n), own, cb.at[g, k, 0, :, cols], agx_s.at[g, n, m], agx_r.at[g, n, m], at_x(k))
        send(("agx", g, n), own, cb.at[g, 0, 1, :, cols], agx_s.at[g, n, 3], agx_r.at[g, n, 3], peer)

    for g in range(GROUPS):
        for n in range(len(CUTS)):
            send_coef(n, g)
    for load in loads:
        load.start()

    lane = lax.broadcasted_iota(jnp.int32, (LOCAL, TRAITS), 1)
    row = lax.broadcasted_iota(jnp.int32, (LOCAL, TRAITS), 0)
    pen_col = jnp.sum(jnp.where(lane == row + ind * LOCAL, pen_ref[...], 0.0), axis=1, keepdims=True)
    s_lane = lax.broadcasted_iota(jnp.int32, (LOCAL, 256), 1)
    s_row = lax.broadcasted_iota(jnp.int32, (LOCAL, 256), 0)

    def add_stat(it, first, column):
        hit = s_lane[: column.shape[0]] == s_row[: column.shape[0]] + first
        stat[it : it + 1, :] += jnp.sum(jnp.where(hit, column, 0.0), axis=0, keepdims=True) * (1.0 / (ROWS * X * C))

    def add_penalty(g, it):
        size = jnp.sum(jnp.abs(bp[g]), axis=1, keepdims=True)
        first = R8 * g
        add_stat(it, ind * LOCAL + first, pen_col[first : first + R8] * (size[:R8] + size[R8:]))

    def t1(n, g, it):
        a, b = CUTS[n]
        cols = pl.ds(a, b - a)
        for m, k in ((1, 1), (2, 3), (0, 2)):
            receive(("agx", g, n), m)
            src, dst = cb.at[g, k, 0, :, cols], cb.at[g, k, 1, :, cols]
            send(("rel", g, n), src, dst, rel_s.at[g, n, m], rel_r.at[g, n, m], peer)
        if n == 1:
            add_penalty(g, it)

    def t2(n, g, it):
        if n == 0:
            for part in range(len(CUTS)):
                receive(("agx", g, part), 3)
                receive(("rel", g, part))
            settle(("rsy", g))
            for k in range(X):
                a, b = cb[g, k, 0].astype(F32), cb[g, k, 1].astype(F32)
                rows = slice(2 * R8 * k, 2 * R8 * k + 2 * R8)
                coef[g, rows, :LO] = jnp.concatenate([a[:R8], b[:R8]], axis=0).astype(BF16)
                coef[g, rows, LO:] = jnp.concatenate([a[R8:, :HI], b[R8:, :HI]], axis=0).astype(BF16)
        k = (2, 1, 3, 0)[n]
        if it == 0 and not loaded[n]:
            loads[n].wait()
            loaded[n] = True
        mine = lax.dot_general(
            coef[g], g_buf[CHUNK * k : CHUNK * k + CHUNK, :], NT, preferred_element_type=F32
        )
        if it:
            mine = mine - pp[g, k]
        if it and k:
            pph[g, k - 1] = mine.astype(BF16)
        else:
            pp[g, k] = mine
        if k:
            src, dst = (pph.at[g, k - 1], ryh.at[g, k - 1]) if it else (pp.at[g, k], ry.at[g, k - 1])
            send(("rsy", g), src, dst, rsy_s.at[g, k - 1], rsy_r.at[g, k - 1], at_y(k))

    def t3(g, it):
        receive(("rsy", g))
        settle(("rsz", g))
        total = pp[g, 0]
        for k in range(Y - 1):
            total = total + (ryh[g, k].astype(F32) if it else ry[g, k])
        sz[g] = total.reshape(Z, R8, CHUNK)
        for k in NEAR_Z:
            send(("rsz", g), sz.at[g, (z + k) % Z], rz.at[g, k - 1], rsz_s.at[g, k - 1], rsz_r.at[g, k - 1], at_z(k))

    def t4(g, it):
        if it == 0 and not ph_loaded:
            ph_load.wait()
            ph_loaded.append(True)
        receive(("rsz", g))
        settle(("agz", g))
        total = sz[g, z]
        for k in range(Z - 1):
            total = total + rz[g, k]
        if it:
            total = total + keep[g]
        else:
            keep[g] = total
        k, f = z // C, z % C
        owner = ((x - k + X) % X) * C + (c + f) % C
        first = owner * LOCAL + R8 * g
        residual = ph_t[pl.ds(pl.multiple_of(first, R8), R8), :] - total
        az[g, z] = residual
        for k in NEAR_Z:
            send(("agz", g), az.at[g, z], az.at[g, z], agz_s.at[g, k - 1], agz_r.at[g, k - 1], at_z(k))
        add_stat(it, first, 0.5 * jnp.sum(residual * residual, axis=1, keepdims=True))

    def t5(g, it):
        receive(("agz", g))
        settle(("agy", g))
        rt[g, :, :CHUNK] = az[g].reshape(GT, CHUNK).astype(BF16)
        for k in (2, 1, 3):
            m = (Y - k) % Y
            send(
                ("agy", g), rt.at[g, :, pl.ds(0, CHUNK)], rt.at[g, :, pl.ds(m * CHUNK, CHUNK)],
                agy_s.at[g, k - 1], agy_r.at[g, k - 1], at_y(k),
            )

    def t6(n, g, it):
        if n == 0:
            receive(("agy", g))
        row, part = n % 2, n // 2
        a, b = CUTS[part]
        high = min(b, HI) if row else b
        if row == 0:
            settle(("pair", g, part))
        grad = lax.dot_general(rt[g], g_buf[:, LO * row + a : LO * row + high], NN, preferred_element_type=F32)
        gp[g, :, :, R8 * row : R8 * row + R8, a:high] = grad.reshape(X, C, R8, high - a)
        if row:
            cols = pl.ds(a, b - a)
            src, dst = gp.at[g, :, 1, :, cols], pr.at[g, :, :, cols]
            send(("pair", g, part), src, dst, pair_s.at[g, part], pair_r.at[g, part], peer)

    def t7(n, g, it):
        a, b = CUTS[n]
        cols = pl.ds(a, b - a)
        receive(("pair", g, n))
        settle(("rel", g, n))
        settle(("rsx", g, n))
        for k in (2, 1, 3, 0):
            mine = gp[g, k, 0, :, a:b] + pr[g, k, :, a:b]
            if it:
                mine = mine - ps[g, k, :, a:b]
            if it and k:
                psh[g, k - 1, :, a:b] = mine.astype(BF16)
            else:
                ps[g, k, :, a:b] = mine
            if k:
                src = psh.at[g, k - 1, :, cols] if it else ps.at[g, k, :, cols]
                dst = (rxh if it else rx).at[g, k - 1, :, cols]
                send(("rsx", g, n), src, dst, rsx_s.at[g, n, k - 1], rsx_r.at[g, n, k - 1], at_x(X - k))

    def t8(n, g, it):
        a, b = CUTS[n]
        high = min(b, HI)
        receive(("rsx", g, n))
        ascent = ps[g, 0, :, a:b]
        for k in range(X - 1):
            ascent = ascent + (rxh[g, k, :, a:b].astype(F32) if it else rx[g, k, :, a:b])
        if it:
            ascent = ascent + asc[g, :, a:b]
        else:
            asc[g, :, a:b] = ascent
        rows = slice(R8 * g, R8 * g + R8)
        moved = bp[g, :, a:b] + scale * ascent
        bound = jnp.concatenate([pen_col[rows], pen_col[rows]], axis=0) * scale
        updated = moved - jnp.clip(moved, -bound, bound)
        if it == ITERS - 1:
            out_beta[rows, a:b] = updated[:R8]
            out_beta[rows, LO + a : LO + high] = updated[R8:, : high - a]
        else:
            bp[g, :, a:b] = updated
            send_coef(n, g)

    def o1():
        stat_y[y] = stat[...]
        for k in range(1, Y):
            send("oy", stat_y.at[y], stat_y.at[y], ob_s.at[k - 1], ob_r.at[k - 1], at_y(k))

    def o2():
        receive("oy")
        stat_z[z] = stat_y[0] + stat_y[1] + stat_y[2] + stat_y[3]
        for k in range(1, Z):
            send("oz", stat_z.at[z], stat_z.at[z], ob_s.at[2 + k], ob_r.at[2 + k], at_z(k))

    def o3():
        receive("oz")
        total = stat_z[0]
        for k in range(1, Z):
            total = total + stat_z[k]
        stat_x[x] = total
        for k in range(1, X):
            send("ox", stat_x.at[x], stat_x.at[x], ob_s.at[9 + k], ob_r.at[9 + k], at_x(k))

    def o4():
        receive("ox")
        stat_c[c] = stat_x[0] + stat_x[1] + stat_x[2] + stat_x[3]
        send("oc", stat_c.at[c], stat_c.at[c], ob_s.at[13], ob_r.at[13], peer)

    def o5():
        receive("oc")
        out_obj[...] = (stat_c[0] + stat_c[1])[:ITERS, :TRAITS]

    stages = []
    for it in range(ITERS):
        for stage, parts in ((t1, 2), (t2, Y), (t3, 0), (t4, 0), (t5, 0), (t6, 4), (t7, 2), (t8, 2)):
            stages += [(functools.partial(stage, n), it) for n in range(parts)] or [(stage, it)]
    objective = [o1, o2, o3, o4, o5]
    done = [0] * GROUPS
    for place, g in enumerate(ORDER):
        stage, it = stages[done[g]]
        stage(g, it)
        done[g] += 1
        if min(done) > stages.index((t4, ITERS - 1)) and objective and place % 3 == 0:
            objective.pop(0)()
    for step in objective:
        step()
    for key in list(pending):
        settle(key)


def on_device(genotypes, phenotype, beta_start, penalty, step_size):
    vmem, smem, hbm = (pl.BlockSpec(memory_space=m) for m in (pltpu.VMEM, pltpu.SMEM, pl.ANY))
    dma = pltpu.SemaphoreType.DMA

    def buf(*shape, dtype=F32):
        return pltpu.VMEM(shape, dtype)

    def pairs(*shape):
        return [dma(shape), dma(shape)]

    n, m = GROUPS, len(CUTS)
    return pl.pallas_call(
        kernel,
        name="lasso_steps",
        out_shape=(
            pltpu.VMEM((LOCAL, COLS), F32),
            pltpu.VMEM((ITERS, TRAITS), F32),
        ),
        in_specs=[smem, vmem, hbm, hbm, hbm],
        out_specs=(vmem, vmem),
        scratch_shapes=[
            buf(ROWS, COLS, dtype=BF16),
            buf(TRAITS, CHUNK),
            buf(n, PACK, LO),
            buf(R8, 256),
            buf(Y, R8, 256),
            buf(Z, R8, 256),
            buf(X, R8, 256),
            buf(C, R8, 256),
            buf(n, X, C, PACK, LO, dtype=BF16),
            buf(n, GT, COLS, dtype=BF16),
            buf(n, Y, GT, CHUNK),
            buf(n, Y - 1, GT, CHUNK, dtype=BF16),
            buf(n, Y - 1, GT, CHUNK),
            buf(n, Y - 1, GT, CHUNK, dtype=BF16),
            buf(n, Z, R8, CHUNK),
            buf(n, Z - 1, R8, CHUNK),
            buf(n, Z, R8, CHUNK),
            buf(n, GT, ROWS, dtype=BF16),
            buf(n, R8, CHUNK),
            buf(n, X, C, PACK, LO),
            buf(n, X, PACK, LO),
            buf(n, X, PACK, LO),
            buf(n, X - 1, PACK, LO, dtype=BF16),
            buf(n, X - 1, PACK, LO),
            buf(n, X - 1, PACK, LO, dtype=BF16),
            buf(n, PACK, LO),
            dma((7,)),
            *pairs(n, m, X),
            *pairs(n, m, X - 1),
            *pairs(n, Y - 1),
            *pairs(n, Z - 1),
            *pairs(n, Z - 1),
            *pairs(n, Y - 1),
            *pairs(n, m),
            *pairs(n, m, X - 1),
            *pairs(14),
        ],
        compiler_params=pltpu.CompilerParams(
            collective_id=1, has_side_effects=True, vmem_limit_bytes=55 * 1024 * 1024
        ),
        cost_estimate=pl.CostEstimate(flops=4 * 2 * ROWS * COLS * TRAITS, bytes_accessed=12000000, transcendentals=0),
    )(step_size, penalty.reshape(1, TRAITS), genotypes, phenotype.T, beta_start.reshape(n, R8, COLS))


def solution(mesh):
    placed = (P("ind", "var"), P("ind", None), P("ind", "var"), P(), P())
    return jax.shard_map(
        on_device, mesh=mesh, in_specs=placed, out_specs=(P("ind", "var"), P()), check_vma=False
    )
```

```python
import functools

import jax
import jax.numpy as jnp
from jax import lax
from jax.experimental import pallas as pl
from jax.experimental.pallas import tpu as pltpu
from jax.sharding import PartitionSpec as P

ITERS = 2
X, C, Y, Z = 4, 2, 4, 8
GROUPS = 3
R8 = 8
ROWS, COLS = 1536, 3200
TRAITS = 192
LOCAL = TRAITS // (X * C)
GT = R8 * X * C
CHUNK = ROWS // Y
LO = 1664
HI = COLS - LO
PACK = 2 * R8
CUTS = ((0, 896), (896, LO))
MESH = pl.DeviceIdType.MESH
F32, BF16 = jnp.float32, jnp.bfloat16
NT = (((1,), (1,)), ((), ()))
NN = (((1,), (0,)), ((), ()))
NEAR_Z = (4, 3, 5, 2, 6, 1, 7)
ORDER = (
    0, 0, 1, 0, 1, 0, 0, 0, 2, 2, 1, 0, 2, 2, 1, 2, 2, 0, 1, 1, 2, 1, 0, 2, 0, 0, 0, 1, 0, 0, 2, 0, 1, 0,
    2, 2, 2, 0, 2, 2, 0, 1, 2, 1, 0, 1, 1, 1, 2, 0, 2, 1, 0, 1, 0, 0, 2, 2, 0, 1, 2, 1, 2, 2, 2, 1, 0, 2,
    1, 1, 1, 1, 0, 1, 2, 0, 0, 0, 0, 1, 0, 0, 2, 0, 1, 0, 2, 2, 2, 2, 2, 1, 1, 2, 1, 1, 1, 2, 1, 2, 1, 1,
)


def kernel(
    step_ref, pen_ref, geno, pheno, beta0, out_beta, out_obj,
    g_buf, ph_t, bp, stat, stat_y, stat_z, stat_x, stat_c,
    cb, coef, pp, pph, ry, ryh, sz, rz, az, rt, keep, gp, pr, ps, psh, rx, rxh, asc,
    load_sem,
    agx_s, agx_r, rel_s, rel_r, rsy_s, rsy_r, rsz_s, rsz_r, agz_s, agz_r, agy_s, agy_r, pair_s, pair_r, rsx_s, rsx_r,
    ob_s, ob_r,
):
    ind, var = lax.axis_index("ind"), lax.axis_index("var")
    x, c = ind // C, ind % C
    y, z = var // Z, var % Z

    def at_x(k):
        return (((x + k) % X) * C + c, var)

    def at_y(k):
        return (ind, ((y + k) % Y) * Z + z)

    def at_z(k):
        return (ind, y * Z + (z + k) % Z)

    peer = (x * C + (1 - c), var)

    beta_loads = [
        pltpu.make_async_copy(beta0.at[:, :, pl.ds(0, LO)], bp.at[:, pl.ds(0, R8), :], load_sem.at[0]),
        pltpu.make_async_copy(beta0.at[:, :, pl.ds(LO, HI)], bp.at[:, pl.ds(R8, R8), pl.ds(0, HI)], load_sem.at[1]),
    ]
    for load in beta_loads:
        load.start()
    loads = []
    for n, k in enumerate((2, 1, 3, 0)):
        rows = pl.ds(pl.multiple_of(((y + k) % Y) * CHUNK, CHUNK), CHUNK)
        loads.append(pltpu.make_async_copy(geno.at[rows, :], g_buf.at[pl.ds(k * CHUNK, CHUNK), :], load_sem.at[3 + n]))
    own = pl.ds(pl.multiple_of(y * CHUNK, CHUNK), CHUNK)
    ph_load = pltpu.make_async_copy(pheno.at[:, own], ph_t, load_sem.at[2])
    ph_load.start()

    barrier = pltpu.get_barrier_semaphore()
    partners = [peer]
    partners += [at_x(k) for k in range(1, X)] + [at_y(k) for k in range(1, Y)] + [at_z(k) for k in range(1, Z)]
    for partner in partners:
        pl.semaphore_signal(barrier, inc=1, device_id=partner, device_id_type=MESH)

    scale = step_ref[0]
    bp[:, R8:, HI:] = jnp.zeros((GROUPS, R8, LO - HI), F32)
    for g in range(GROUPS):
        gp[g, :, :, R8:, HI:] = jnp.zeros((X, C, R8, LO - HI), F32)
    stat[...] = jnp.zeros_like(stat)

    pending = {}
    loaded = [False] * Y
    ph_loaded = []

    def send(key, src, dst, s_sem, r_sem, device):
        copy = pltpu.make_async_remote_copy(
            src_ref=src, dst_ref=dst, send_sem=s_sem, recv_sem=r_sem, device_id=device, device_id_type=MESH
        )
        copy.start()
        pending.setdefault(key, []).append(copy)

    def bulk(name, g):
        ref, s_sem, r_sem = (rz.at[g], rsz_s, rsz_r) if name == "rsz" else (az.at[g, pl.ds(0, Z - 1)], agz_s, agz_r)
        return pltpu.make_async_remote_copy(
            src_ref=ref, dst_ref=ref, send_sem=s_sem.at[g], recv_sem=r_sem.at[g], device_id=at_z(1), device_id_type=MESH
        )

    def receive(key, one=None):
        if key[0] in ("rsz", "agz"):
            bulk(*key).wait_recv()
            return
        copies = pending[key] if one is None else [pending[key][one]]
        for copy in copies:
            copy.wait_recv()

    def settle(key):
        copies = pending.pop(key, [])
        if copies and key[0] in ("rsz", "agz"):
            bulk(*key).wait_send()
            return
        for copy in copies:
            copy.wait_send()

    for load in beta_loads:
        load.wait()
    pl.semaphore_wait(barrier, len(partners))

    def send_coef(n, g):
        settle(("agx", g, n))
        a, b = CUTS[n]
        cols = pl.ds(a, b - a)
        cb[g, 0, 0, :, a:b] = bp[g, :, a:b].astype(BF16)
        own = cb.at[g, 0, 0, :, cols]
        for m, k in enumerate((2, 1, 3)):
            send(("agx", g, n), own, cb.at[g, k, 0, :, cols], agx_s.at[g, n, m], agx_r.at[g, n, m], at_x(k))
        send(("agx", g, n), own, cb.at[g, 0, 1, :, cols], agx_s.at[g, n, 3], agx_r.at[g, n, 3], peer)

    for g in range(GROUPS):
        for n in range(len(CUTS)):
            send_coef(n, g)
    for load in loads:
        load.start()

    lane = lax.broadcasted_iota(jnp.int32, (LOCAL, TRAITS), 1)
    row = lax.broadcasted_iota(jnp.int32, (LOCAL, TRAITS), 0)
    pen_col = jnp.sum(jnp.where(lane == row + ind * LOCAL, pen_ref[...], 0.0), axis=1, keepdims=True)
    s_lane = lax.broadcasted_iota(jnp.int32, (LOCAL, 256), 1)
    s_row = lax.broadcasted_iota(jnp.int32, (LOCAL, 256), 0)

    def add_stat(it, first, column):
        hit = s_lane[: column.shape[0]] == s_row[: column.shape[0]] + first
        stat[it : it + 1, :] += jnp.sum(jnp.where(hit, column, 0.0), axis=0, keepdims=True) * (1.0 / (ROWS * X * C))

    def add_penalty(g, it):
        size = jnp.sum(jnp.abs(bp[g]), axis=1, keepdims=True)
        first = R8 * g
        add_stat(it, ind * LOCAL + first, pen_col[first : first + R8] * (size[:R8] + size[R8:]))

    def t1(n, g, it):
        a, b = CUTS[n]
        cols = pl.ds(a, b - a)
        for m, k in ((1, 1), (2, 3), (0, 2)):
            receive(("agx", g, n), m)
            src, dst = cb.at[g, k, 0, :, cols], cb.at[g, k, 1, :, cols]
            send(("rel", g, n), src, dst, rel_s.at[g, n, m], rel_r.at[g, n, m], peer)
        if n == 1:
            add_penalty(g, it)

    def t2(n, g, it):
        if n == 0:
            for part in range(len(CUTS)):
                receive(("agx", g, part), 3)
                receive(("rel", g, part))
            settle(("rsy", g))
            for k in range(X):
                a, b = cb[g, k, 0].astype(F32), cb[g, k, 1].astype(F32)
                rows = slice(2 * R8 * k, 2 * R8 * k + 2 * R8)
                coef[g, rows, :LO] = jnp.concatenate([a[:R8], b[:R8]], axis=0).astype(BF16)
                coef[g, rows, LO:] = jnp.concatenate([a[R8:, :HI], b[R8:, :HI]], axis=0).astype(BF16)
        k = (2, 1, 3, 0)[n]
        if it == 0 and not loaded[n]:
            loads[n].wait()
            loaded[n] = True
        mine = lax.dot_general(
            coef[g], g_buf[CHUNK * k : CHUNK * k + CHUNK, :], NT, preferred_element_type=F32
        )
        if it:
            mine = mine - pp[g, k]
        if it and k:
            pph[g, k - 1] = mine.astype(BF16)
        else:
            pp[g, k] = mine
        if k:
            src, dst = (pph.at[g, k - 1], ryh.at[g, k - 1]) if it else (pp.at[g, k], ry.at[g, k - 1])
            send(("rsy", g), src, dst, rsy_s.at[g, k - 1], rsy_r.at[g, k - 1], at_y(k))

    def t3(g, it):
        receive(("rsy", g))
        settle(("rsz", g))
        total = pp[g, 0]
        for k in range(Y - 1):
            total = total + (ryh[g, k].astype(F32) if it else ry[g, k])
        sz[g] = total.reshape(Z, R8, CHUNK)
        for k in NEAR_Z:
            send(("rsz", g), sz.at[g, (z + k) % Z], rz.at[g, k - 1], rsz_s.at[g], rsz_r.at[g], at_z(k))

    def t4(g, it):
        if it == 0 and not ph_loaded:
            ph_load.wait()
            ph_loaded.append(True)
        receive(("rsz", g))
        settle(("agz", g))
        total = sz[g, z]
        for k in range(Z - 1):
            total = total + rz[g, k]
        if it:
            total = total + keep[g]
        else:
            keep[g] = total
        k, f = z // C, z % C
        owner = ((x - k + X) % X) * C + (c + f) % C
        first = owner * LOCAL + R8 * g
        residual = ph_t[pl.ds(pl.multiple_of(first, R8), R8), :] - total
        az[g, z] = residual
        for k in NEAR_Z:
            send(("agz", g), az.at[g, z], az.at[g, z], agz_s.at[g], agz_r.at[g], at_z(k))
        add_stat(it, first, 0.5 * jnp.sum(residual * residual, axis=1, keepdims=True))

    def t5(g, it):
        receive(("agz", g))
        settle(("agy", g))
        rt[g, :, :CHUNK] = az[g].reshape(GT, CHUNK).astype(BF16)
        for k in (2, 1, 3):
            m = (Y - k) % Y
            send(
                ("agy", g), rt.at[g, :, pl.ds(0, CHUNK)], rt.at[g, :, pl.ds(m * CHUNK, CHUNK)],
                agy_s.at[g, k - 1], agy_r.at[g, k - 1], at_y(k),
            )

    def t6(n, g, it):
        if n == 0:
            receive(("agy", g))
        row, part = n % 2, n // 2
        a, b = CUTS[part]
        high = min(b, HI) if row else b
        if row == 0:
            settle(("pair", g, part))
        grad = lax.dot_general(rt[g], g_buf[:, LO * row + a : LO * row + high], NN, preferred_element_type=F32)
        gp[g, :, :, R8 * row : R8 * row + R8, a:high] = grad.reshape(X, C, R8, high - a)
        if row:
            cols = pl.ds(a, b - a)
            src, dst = gp.at[g, :, 1, :, cols], pr.at[g, :, :, cols]
            send(("pair", g, part), src, dst, pair_s.at[g, part], pair_r.at[g, part], peer)

    def t7(n, g, it):
        a, b = CUTS[n]
        cols = pl.ds(a, b - a)
        receive(("pair", g, n))
        settle(("rel", g, n))
        settle(("rsx", g, n))
        for k in (2, 1, 3, 0):
            mine = gp[g, k, 0, :, a:b] + pr[g, k, :, a:b]
            if it:
                mine = mine - ps[g, k, :, a:b]
            if it and k:
                psh[g, k - 1, :, a:b] = mine.astype(BF16)
            else:
                ps[g, k, :, a:b] = mine
            if k:
                src = psh.at[g, k - 1, :, cols] if it else ps.at[g, k, :, cols]
                dst = (rxh if it else rx).at[g, k - 1, :, cols]
                send(("rsx", g, n), src, dst, rsx_s.at[g, n, k - 1], rsx_r.at[g, n, k - 1], at_x(X - k))

    def t8(n, g, it):
        a, b = CUTS[n]
        high = min(b, HI)
        receive(("rsx", g, n))
        ascent = ps[g, 0, :, a:b]
        for k in range(X - 1):
            ascent = ascent + (rxh[g, k, :, a:b].astype(F32) if it else rx[g, k, :, a:b])
        if it:
            ascent = ascent + asc[g, :, a:b]
        else:
            asc[g, :, a:b] = ascent
        rows = slice(R8 * g, R8 * g + R8)
        moved = bp[g, :, a:b] + scale * ascent
        bound = jnp.concatenate([pen_col[rows], pen_col[rows]], axis=0) * scale
        updated = moved - jnp.clip(moved, -bound, bound)
        if it == ITERS - 1:
            out_beta[rows, a:b] = updated[:R8]
            out_beta[rows, LO + a : LO + high] = updated[R8:, : high - a]
        else:
            bp[g, :, a:b] = updated
            send_coef(n, g)

    def o1():
        stat_y[y] = stat[...]
        for k in range(1, Y):
            send("oy", stat_y.at[y], stat_y.at[y], ob_s.at[k - 1], ob_r.at[k - 1], at_y(k))

    def o2():
        receive("oy")
        stat_z[z] = stat_y[0] + stat_y[1] + stat_y[2] + stat_y[3]
        for k in range(1, Z):
            send("oz", stat_z.at[z], stat_z.at[z], ob_s.at[2 + k], ob_r.at[2 + k], at_z(k))

    def o3():
        receive("oz")
        total = stat_z[0]
        for k in range(1, Z):
            total = total + stat_z[k]
        stat_x[x] = total
        for k in range(1, X):
            send("ox", stat_x.at[x], stat_x.at[x], ob_s.at[9 + k], ob_r.at[9 + k], at_x(k))

    def o4():
        receive("ox")
        stat_c[c] = stat_x[0] + stat_x[1] + stat_x[2] + stat_x[3]
        send("oc", stat_c.at[c], stat_c.at[c], ob_s.at[13], ob_r.at[13], peer)

    def o5():
        receive("oc")
        out_obj[...] = (stat_c[0] + stat_c[1])[:ITERS, :TRAITS]

    stages = []
    for it in range(ITERS):
        for stage, parts in ((t1, 2), (t2, Y), (t3, 0), (t4, 0), (t5, 0), (t6, 4), (t7, 2), (t8, 2)):
            stages += [(functools.partial(stage, n), it) for n in range(parts)] or [(stage, it)]
    objective = [o1, o2, o3, o4, o5]
    done = [0] * GROUPS
    for place, g in enumerate(ORDER):
        stage, it = stages[done[g]]
        stage(g, it)
        done[g] += 1
        if min(done) > stages.index((t4, ITERS - 1)) and objective and place % 3 == 0:
            objective.pop(0)()
    for step in objective:
        step()
    for key in list(pending):
        settle(key)


def on_device(genotypes, phenotype, beta_start, penalty, step_size):
    vmem, smem, hbm = (pl.BlockSpec(memory_space=m) for m in (pltpu.VMEM, pltpu.SMEM, pl.ANY))
    dma = pltpu.SemaphoreType.DMA

    def buf(*shape, dtype=F32):
        return pltpu.VMEM(shape, dtype)

    def pairs(*shape):
        return [dma(shape), dma(shape)]

    n, m = GROUPS, len(CUTS)
    return pl.pallas_call(
        kernel,
        name="lasso_steps",
        out_shape=(
            pltpu.VMEM((LOCAL, COLS), F32),
            pltpu.VMEM((ITERS, TRAITS), F32),
        ),
        in_specs=[smem, vmem, hbm, hbm, hbm],
        out_specs=(vmem, vmem),
        scratch_shapes=[
            buf(ROWS, COLS, dtype=BF16),
            buf(TRAITS, CHUNK),
            buf(n, PACK, LO),
            buf(R8, 256),
            buf(Y, R8, 256),
            buf(Z, R8, 256),
            buf(X, R8, 256),
            buf(C, R8, 256),
            buf(n, X, C, PACK, LO, dtype=BF16),
            buf(n, GT, COLS, dtype=BF16),
            buf(n, Y, GT, CHUNK),
            buf(n, Y - 1, GT, CHUNK, dtype=BF16),
            buf(n, Y - 1, GT, CHUNK),
            buf(n, Y - 1, GT, CHUNK, dtype=BF16),
            buf(n, Z, R8, CHUNK),
            buf(n, Z - 1, R8, CHUNK),
            buf(n, Z, R8, CHUNK),
            buf(n, GT, ROWS, dtype=BF16),
            buf(n, R8, CHUNK),
            buf(n, X, C, PACK, LO),
            buf(n, X, PACK, LO),
            buf(n, X, PACK, LO),
            buf(n, X - 1, PACK, LO, dtype=BF16),
            buf(n, X - 1, PACK, LO),
            buf(n, X - 1, PACK, LO, dtype=BF16),
            buf(n, PACK, LO),
            dma((7,)),
            *pairs(n, m, X),
            *pairs(n, m, X - 1),
            *pairs(n, Y - 1),
            *pairs(n),
            *pairs(n),
            *pairs(n, Y - 1),
            *pairs(n, m),
            *pairs(n, m, X - 1),
            *pairs(14),
        ],
        compiler_params=pltpu.CompilerParams(
            collective_id=1, has_side_effects=True, vmem_limit_bytes=55 * 1024 * 1024
        ),
        cost_estimate=pl.CostEstimate(flops=4 * 2 * ROWS * COLS * TRAITS, bytes_accessed=12000000, transcendentals=0),
    )(step_size, penalty.reshape(1, TRAITS), genotypes, phenotype.T, beta_start.reshape(n, R8, COLS))


def solution(mesh):
    placed = (P("ind", "var"), P("ind", None), P("ind", "var"), P(), P())
    return jax.shard_map(
        on_device, mesh=mesh, in_specs=placed, out_specs=(P("ind", "var"), P()), check_vma=False
    )
```

```python
import functools

import jax
import jax.numpy as jnp
from jax import lax
from jax.experimental import pallas as pl
from jax.experimental.pallas import tpu as pltpu
from jax.sharding import PartitionSpec as P

ITERS = 2
X, C, Y, Z = 4, 2, 4, 8
GROUPS = 3
R8 = 8
ROWS, COLS = 1536, 3200
TRAITS = 192
LOCAL = TRAITS // (X * C)
GT = R8 * X * C
CHUNK = ROWS // Y
LO = 1664
HI = COLS - LO
PACK = 2 * R8
CUTS = ((0, 896), (896, LO))
MESH = pl.DeviceIdType.MESH
F32, BF16 = jnp.float32, jnp.bfloat16
NT = (((1,), (1,)), ((), ()))
NN = (((1,), (0,)), ((), ()))
NEAR_Z = (4, 3, 5, 2, 6, 1, 7)
ORDER = (
    0, 0, 1, 0, 1, 0, 0, 0, 2, 2, 1, 0, 2, 2, 1, 2, 2, 0, 1, 1, 2, 1, 0, 2, 0, 0, 0, 1, 0, 0, 2, 0, 1, 0,
    2, 2, 2, 0, 2, 2, 0, 1, 2, 1, 0, 1, 1, 1, 2, 0, 2, 1, 0, 1, 0, 0, 2, 2, 0, 1, 2, 1, 2, 2, 2, 1, 0, 2,
    1, 1, 1, 1, 0, 1, 2, 0, 0, 0, 0, 1, 0, 0, 2, 0, 1, 0, 2, 2, 2, 2, 2, 1, 1, 2, 1, 1, 1, 2, 1, 2, 1, 1,
)


def kernel(
    step_ref, pen_ref, geno, pheno, beta0, out_beta, out_obj,
    g_buf, ph_t, bp, stat, stat_y, stat_z, stat_x, stat_c,
    cb, coef, pp, pph, ry, ryh, sz, rz, az, rt, keep, gp, pr, ps, psh, rx, rxh, asc,
    load_sem,
    agx_s, agx_r, rel_s, rel_r, rsy_s, rsy_r, rsz_s, rsz_r, agz_s, agz_r, agy_s, agy_r, pair_s, pair_r, rsx_s, rsx_r,
    ob_s, ob_r,
):
    ind, var = lax.axis_index("ind"), lax.axis_index("var")
    x, c = ind // C, ind % C
    y, z = var // Z, var % Z

    def at_x(k):
        return (((x + k) % X) * C + c, var)

    def at_y(k):
        return (ind, ((y + k) % Y) * Z + z)

    def at_z(k):
        return (ind, y * Z + (z + k) % Z)

    peer = (x * C + (1 - c), var)

    beta_loads = [
        pltpu.make_async_copy(beta0.at[:, :, pl.ds(0, LO)], bp.at[:, pl.ds(0, R8), :], load_sem.at[0]),
        pltpu.make_async_copy(beta0.at[:, :, pl.ds(LO, HI)], bp.at[:, pl.ds(R8, R8), pl.ds(0, HI)], load_sem.at[1]),
    ]
    for load in beta_loads:
        load.start()
    loads = []
    for n, k in enumerate((2, 1, 3, 0)):
        rows = pl.ds(pl.multiple_of(((y + k) % Y) * CHUNK, CHUNK), CHUNK)
        loads.append(pltpu.make_async_copy(geno.at[rows, :], g_buf.at[pl.ds(k * CHUNK, CHUNK), :], load_sem.at[3 + n]))
    own = pl.ds(pl.multiple_of(y * CHUNK, CHUNK), CHUNK)
    ph_load = pltpu.make_async_copy(pheno.at[:, own], ph_t, load_sem.at[2])
    ph_load.start()

    barrier = pltpu.get_barrier_semaphore()
    partners = [peer]
    partners += [at_x(k) for k in range(1, X)] + [at_y(k) for k in range(1, Y)] + [at_z(k) for k in range(1, Z)]
    for partner in partners:
        pl.semaphore_signal(barrier, inc=1, device_id=partner, device_id_type=MESH)

    scale = step_ref[0]
    bp[:, R8:, HI:] = jnp.zeros((GROUPS, R8, LO - HI), F32)
    for g in range(GROUPS):
        gp[g, :, :, R8:, HI:] = jnp.zeros((X, C, R8, LO - HI), F32)
    stat[...] = jnp.zeros_like(stat)

    pending = {}
    loaded = [False] * Y
    ph_loaded = []

    def send(key, src, dst, s_sem, r_sem, device):
        copy = pltpu.make_async_remote_copy(
            src_ref=src, dst_ref=dst, send_sem=s_sem, recv_sem=r_sem, device_id=device, device_id_type=MESH
        )
        copy.start()
        pending.setdefault(key, []).append(copy)

    def bulk(name, g):
        ref, s_sem, r_sem = (rz.at[g], rsz_s, rsz_r) if name == "rsz" else (az.at[g, pl.ds(0, Z - 1)], agz_s, agz_r)
        return pltpu.make_async_remote_copy(
            src_ref=ref, dst_ref=ref, send_sem=s_sem.at[g], recv_sem=r_sem.at[g], device_id=at_z(1), device_id_type=MESH
        )

    def receive(key, one=None):
        if key[0] in ("rsz", "agz"):
            bulk(*key).wait_recv()
            return
        copies = pending[key] if one is None else [pending[key][one]]
        for copy in copies:
            copy.wait_recv()

    def settle(key):
        copies = pending.pop(key, [])
        if copies and key[0] in ("rsz", "agz"):
            bulk(*key).wait_send()
            return
        for copy in copies:
            copy.wait_send()

    for load in beta_loads:
        load.wait()
    pl.semaphore_wait(barrier, len(partners))

    def send_coef(n, g):
        settle(("agx", g, n))
        a, b = CUTS[n]
        cols = pl.ds(a, b - a)
        cb[g, 0, 0, :, a:b] = bp[g, :, a:b].astype(BF16)
        own = cb.at[g, 0, 0, :, cols]
        for m, k in enumerate((2, 1, 3)):
            send(("agx", g, n), own, cb.at[g, k, 0, :, cols], agx_s.at[g, n, m], agx_r.at[g, n, m], at_x(k))
        send(("agx", g, n), own, cb.at[g, 0, 1, :, cols], agx_s.at[g, n, 3], agx_r.at[g, n, 3], peer)

    for g in range(GROUPS):
        for n in range(len(CUTS)):
            send_coef(n, g)
    for load in loads:
        load.start()

    lane = lax.broadcasted_iota(jnp.int32, (LOCAL, TRAITS), 1)
    row = lax.broadcasted_iota(jnp.int32, (LOCAL, TRAITS), 0)
    pen_col = jnp.sum(jnp.where(lane == row + ind * LOCAL, pen_ref[...], 0.0), axis=1, keepdims=True)
    s_lane = lax.broadcasted_iota(jnp.int32, (LOCAL, 256), 1)
    s_row = lax.broadcasted_iota(jnp.int32, (LOCAL, 256), 0)

    def add_stat(it, first, column):
        hit = s_lane[: column.shape[0]] == s_row[: column.shape[0]] + first
        stat[it : it + 1, :] += jnp.sum(jnp.where(hit, column, 0.0), axis=0, keepdims=True) * (1.0 / (ROWS * X * C))

    def add_penalty(g, it):
        size = jnp.sum(jnp.abs(bp[g]), axis=1, keepdims=True)
        first = R8 * g
        add_stat(it, ind * LOCAL + first, pen_col[first : first + R8] * (size[:R8] + size[R8:]))

    def t1(n, g, it):
        a, b = CUTS[n]
        cols = pl.ds(a, b - a)
        for m in range(X - 1):
            receive(("agx", g, n), m)
        others = pl.ds(1, X - 1)
        src, dst = cb.at[g, others, 0, :, cols], cb.at[g, others, 1, :, cols]
        send(("rel", g, n), src, dst, rel_s.at[g, n], rel_r.at[g, n], peer)
        if n == 1:
            add_penalty(g, it)

    def t2(n, g, it):
        if n == 0:
            for part in range(len(CUTS)):
                receive(("agx", g, part), 3)
                receive(("rel", g, part))
            settle(("rsy", g))
            for k in range(X):
                a, b = cb[g, k, 0].astype(F32), cb[g, k, 1].astype(F32)
                rows = slice(2 * R8 * k, 2 * R8 * k + 2 * R8)
                coef[g, rows, :LO] = jnp.concatenate([a[:R8], b[:R8]], axis=0).astype(BF16)
                coef[g, rows, LO:] = jnp.concatenate([a[R8:, :HI], b[R8:, :HI]], axis=0).astype(BF16)
        k = (2, 1, 3, 0)[n]
        if it == 0 and not loaded[n]:
            loads[n].wait()
            loaded[n] = True
        mine = lax.dot_general(
            coef[g], g_buf[CHUNK * k : CHUNK * k + CHUNK, :], NT, preferred_element_type=F32
        )
        if it:
            mine = mine - pp[g, k]
        if it and k:
            pph[g, k - 1] = mine.astype(BF16)
        else:
            pp[g, k] = mine
        if k:
            src, dst = (pph.at[g, k - 1], ryh.at[g, k - 1]) if it else (pp.at[g, k], ry.at[g, k - 1])
            send(("rsy", g), src, dst, rsy_s.at[g, k - 1], rsy_r.at[g, k - 1], at_y(k))

    def t3(g, it):
        receive(("rsy", g))
        settle(("rsz", g))
        total = pp[g, 0]
        for k in range(Y - 1):
            total = total + (ryh[g, k].astype(F32) if it else ry[g, k])
        sz[g] = total.reshape(Z, R8, CHUNK)
        for k in NEAR_Z:
            send(("rsz", g), sz.at[g, (z + k) % Z], rz.at[g, k - 1], rsz_s.at[g], rsz_r.at[g], at_z(k))

    def t4(g, it):
        if it == 0 and not ph_loaded:
            ph_load.wait()
            ph_loaded.append(True)
        receive(("rsz", g))
        settle(("agz", g))
        total = sz[g, z]
        for k in range(Z - 1):
            total = total + rz[g, k]
        if it:
            total = total + keep[g]
        else:
            keep[g] = total
        k, f = z // C, z % C
        owner = ((x - k + X) % X) * C + (c + f) % C
        first = owner * LOCAL + R8 * g
        residual = ph_t[pl.ds(pl.multiple_of(first, R8), R8), :] - total
        az[g, z] = residual
        for k in NEAR_Z:
            send(("agz", g), az.at[g, z], az.at[g, z], agz_s.at[g], agz_r.at[g], at_z(k))
        add_stat(it, first, 0.5 * jnp.sum(residual * residual, axis=1, keepdims=True))

    def t5(g, it):
        receive(("agz", g))
        settle(("agy", g))
        rt[g, :, :CHUNK] = az[g].reshape(GT, CHUNK).astype(BF16)
        for k in (2, 1, 3):
            m = (Y - k) % Y
            send(
                ("agy", g), rt.at[g, :, pl.ds(0, CHUNK)], rt.at[g, :, pl.ds(m * CHUNK, CHUNK)],
                agy_s.at[g, k - 1], agy_r.at[g, k - 1], at_y(k),
            )

    def t6(n, g, it):
        if n == 0:
            receive(("agy", g))
        row, part = n % 2, n // 2
        a, b = CUTS[part]
        high = min(b, HI) if row else b
        if row == 0:
            settle(("pair", g, part))
        grad = lax.dot_general(rt[g], g_buf[:, LO * row + a : LO * row + high], NN, preferred_element_type=F32)
        gp[g, :, :, R8 * row : R8 * row + R8, a:high] = grad.reshape(X, C, R8, high - a)
        if row:
            cols = pl.ds(a, b - a)
            src, dst = gp.at[g, :, 1, :, cols], pr.at[g, :, :, cols]
            send(("pair", g, part), src, dst, pair_s.at[g, part], pair_r.at[g, part], peer)

    def t7(n, g, it):
        a, b = CUTS[n]
        cols = pl.ds(a, b - a)
        receive(("pair", g, n))
        settle(("rel", g, n))
        settle(("rsx", g, n))
        for k in (2, 1, 3, 0):
            mine = gp[g, k, 0, :, a:b] + pr[g, k, :, a:b]
            if it:
                mine = mine - ps[g, k, :, a:b]
            if it and k:
                psh[g, k - 1, :, a:b] = mine.astype(BF16)
            else:
                ps[g, k, :, a:b] = mine
            if k:
                src = psh.at[g, k - 1, :, cols] if it else ps.at[g, k, :, cols]
                dst = (rxh if it else rx).at[g, k - 1, :, cols]
                send(("rsx", g, n), src, dst, rsx_s.at[g, n, k - 1], rsx_r.at[g, n, k - 1], at_x(X - k))

    def t8(n, g, it):
        a, b = CUTS[n]
        high = min(b, HI)
        receive(("rsx", g, n))
        ascent = ps[g, 0, :, a:b]
        for k in range(X - 1):
            ascent = ascent + (rxh[g, k, :, a:b].astype(F32) if it else rx[g, k, :, a:b])
        if it:
            ascent = ascent + asc[g, :, a:b]
        else:
            asc[g, :, a:b] = ascent
        rows = slice(R8 * g, R8 * g + R8)
        moved = bp[g, :, a:b] + scale * ascent
        bound = jnp.concatenate([pen_col[rows], pen_col[rows]], axis=0) * scale
        updated = moved - jnp.clip(moved, -bound, bound)
        if it == ITERS - 1:
            out_beta[rows, a:b] = updated[:R8]
            out_beta[rows, LO + a : LO + high] = updated[R8:, : high - a]
        else:
            bp[g, :, a:b] = updated
            send_coef(n, g)

    def o1():
        stat_y[y] = stat[...]
        for k in range(1, Y):
            send("oy", stat_y.at[y], stat_y.at[y], ob_s.at[k - 1], ob_r.at[k - 1], at_y(k))

    def o2():
        receive("oy")
        stat_z[z] = stat_y[0] + stat_y[1] + stat_y[2] + stat_y[3]
        for k in range(1, Z):
            send("oz", stat_z.at[z], stat_z.at[z], ob_s.at[2 + k], ob_r.at[2 + k], at_z(k))

    def o3():
        receive("oz")
        total = stat_z[0]
        for k in range(1, Z):
            total = total + stat_z[k]
        stat_x[x] = total
        for k in range(1, X):
            send("ox", stat_x.at[x], stat_x.at[x], ob_s.at[9 + k], ob_r.at[9 + k], at_x(k))

    def o4():
        receive("ox")
        stat_c[c] = stat_x[0] + stat_x[1] + stat_x[2] + stat_x[3]
        send("oc", stat_c.at[c], stat_c.at[c], ob_s.at[13], ob_r.at[13], peer)

    def o5():
        receive("oc")
        out_obj[...] = (stat_c[0] + stat_c[1])[:ITERS, :TRAITS]

    stages = []
    for it in range(ITERS):
        for stage, parts in ((t1, 2), (t2, Y), (t3, 0), (t4, 0), (t5, 0), (t6, 4), (t7, 2), (t8, 2)):
            stages += [(functools.partial(stage, n), it) for n in range(parts)] or [(stage, it)]
    objective = [o1, o2, o3, o4, o5]
    done = [0] * GROUPS
    for place, g in enumerate(ORDER):
        stage, it = stages[done[g]]
        stage(g, it)
        done[g] += 1
        if min(done) > stages.index((t4, ITERS - 1)) and objective and place % 3 == 0:
            objective.pop(0)()
    for step in objective:
        step()
    for key in list(pending):
        settle(key)


def on_device(genotypes, phenotype, beta_start, penalty, step_size):
    vmem, smem, hbm = (pl.BlockSpec(memory_space=m) for m in (pltpu.VMEM, pltpu.SMEM, pl.ANY))
    dma = pltpu.SemaphoreType.DMA

    def buf(*shape, dtype=F32):
        return pltpu.VMEM(shape, dtype)

    def pairs(*shape):
        return [dma(shape), dma(shape)]

    n, m = GROUPS, len(CUTS)
    return pl.pallas_call(
        kernel,
        name="lasso_steps",
        out_shape=(
            pltpu.VMEM((LOCAL, COLS), F32),
            pltpu.VMEM((ITERS, TRAITS), F32),
        ),
        in_specs=[smem, vmem, hbm, hbm, hbm],
        out_specs=(vmem, vmem),
        scratch_shapes=[
            buf(ROWS, COLS, dtype=BF16),
            buf(TRAITS, CHUNK),
            buf(n, PACK, LO),
            buf(R8, 256),
            buf(Y, R8, 256),
            buf(Z, R8, 256),
            buf(X, R8, 256),
            buf(C, R8, 256),
            buf(n, X, C, PACK, LO, dtype=BF16),
            buf(n, GT, COLS, dtype=BF16),
            buf(n, Y, GT, CHUNK),
            buf(n, Y - 1, GT, CHUNK, dtype=BF16),
            buf(n, Y - 1, GT, CHUNK),
            buf(n, Y - 1, GT, CHUNK, dtype=BF16),
            buf(n, Z, R8, CHUNK),
            buf(n, Z - 1, R8, CHUNK),
            buf(n, Z, R8, CHUNK),
            buf(n, GT, ROWS, dtype=BF16),
            buf(n, R8, CHUNK),
            buf(n, X, C, PACK, LO),
            buf(n, X, PACK, LO),
            buf(n, X, PACK, LO),
            buf(n, X - 1, PACK, LO, dtype=BF16),
            buf(n, X - 1, PACK, LO),
            buf(n, X - 1, PACK, LO, dtype=BF16),
            buf(n, PACK, LO),
            dma((7,)),
            *pairs(n, m, X),
            *pairs(n, m),
            *pairs(n, Y - 1),
            *pairs(n),
            *pairs(n),
            *pairs(n, Y - 1),
            *pairs(n, m),
            *pairs(n, m, X - 1),
            *pairs(14),
        ],
        compiler_params=pltpu.CompilerParams(
            collective_id=1, has_side_effects=True, vmem_limit_bytes=55 * 1024 * 1024
        ),
        cost_estimate=pl.CostEstimate(flops=4 * 2 * ROWS * COLS * TRAITS, bytes_accessed=12000000, transcendentals=0),
    )(step_size, penalty.reshape(1, TRAITS), genotypes, phenotype.T, beta_start.reshape(n, R8, COLS))


def solution(mesh):
    placed = (P("ind", "var"), P("ind", None), P("ind", "var"), P(), P())
    return jax.shard_map(
        on_device, mesh=mesh, in_specs=placed, out_specs=(P("ind", "var"), P()), check_vma=False
    )
```
